32 devices in a mesh: band: 8 (over z, y), ga: 4 (over x, core).
Axes of the slice: x: 2, y: 2, z: 4, core: 2. Of those that a mesh axis runs over, the one named last changes fastest.
Arguments:
- valence: bfloat16 [8, 2, 128, 128, 128], P('band', None, 'ga'), may hold values from -6 to 6
- conduction: bfloat16 [48, 128, 128, 128], P('band', 'ga'), may hold values from -6 to 6
- owners: int32 [2], replicated, may hold values from 0 to 7
- val_energy: float32 [2], replicated, may hold values from -8 to -4
- cond_energy: float32 [48], P('band'), may hold values from 0.5 to 20
- gvec_index: int32 [1280], P('ga'), may hold values from 0 to 65535, as said below
Outputs:
- chi_panel: float32 [1280, 512], P('band', 'ga')
The draws below stay inside these ranges and needn't reach their ends.
Inputs may be any that keep to these rules, and one draw needn't show every extreme that they name: owners[k] is the band group whose slot k holds valence band k. `gvec_index`: within each block j of 320 entries the values are distinct; value a 1024 + b * 64 + c names x-frequency index a, y-frequency index j * 16 + b, z-frequency index c.
All inputs are finite; a program needn't handle non-finite values.
Results may differ from the reference program's by a relative error of at most 0.0048.
Values may be sent and summed in bfloat16 or wider, within the bound.
No kernel may reach another device: no remote copies, remote signals or barrier semaphores. Data moves between devices by JAX's collectives and lax.ppermute only.
A program may use at most 128 MiB of HBM per device.

```python
import math
import jax
import jax.numpy as jnp
from jax import lax

NGRID = 128
KB = 64
NV = 2
NGD = 320
PANEL_DEV = 128
KYD = 16
GCELLS = 65536
NG = 1280
CBANDS = 48
N_BAND = 8
N_GA = 4


def draw_gvec_index(key, part):

    def one_block(block_key):
        inner = jax.random.permutation(jax.random.fold_in(block_key, 1), GCELLS - 2)[:NGD - 2] + 1
        ends = jnp.array([0, GCELLS - 1], dtype=jnp.int32)
        joined = jnp.concatenate([inner.astype(jnp.int32), ends])
        order = jax.random.permutation(jax.random.fold_in(block_key, 2), NGD)
        return joined[order]
    block_numbers = jnp.arange(NG // NGD)
    block_keys = jax.vmap(lambda number: jax.random.fold_in(key, number))(block_numbers)
    return jax.vmap(one_block)(block_keys).reshape(NG)


def block_levels(rng, shape, split, least, high):
    loudness = 1.0
    for dim, blocks in split:
        heights = jax.random.uniform(jax.random.fold_in(jax.random.fold_in(rng, 6), dim), (blocks,), jnp.float32, least / len(split), high / len(split))
        loudness = loudness * jnp.repeat(jnp.exp(heights), shape[dim] // blocks).reshape((-1,) + (1,) * (len(shape) - 1 - dim))
    return loudness


def gaussian(rng, extent, deviation, most, split=(), kind=jnp.bfloat16):
    values = deviation * jax.random.normal(rng, extent, jnp.float32)
    if split:
        values = values * block_levels(rng, extent, split, -0.22, 0.18)
    return jnp.clip(values, -most, most).astype(kind)


def setup_inputs(seed: int = 0) -> dict:
    streams_of = jax.random.split(jax.random.key(seed), 7)
    return {
        "valence": gaussian(streams_of[0], (N_BAND, NV, NGRID, NGRID, NGRID), 1.0, 6.0, ((0, 8), (2, 4))),
        "conduction": gaussian(streams_of[1], (CBANDS, NGRID, NGRID, NGRID), 1.0, 6.0, ((0, 8), (1, 4))),
        "owners": jax.random.randint(streams_of[2], (NV,), 0, N_BAND).astype(jnp.int32),
        "val_energy": jnp.clip(jax.random.uniform(streams_of[3], (NV,), jnp.float32, -8.0, -4.0), -8.0, -4.0),
        "cond_energy": jnp.clip(0.5 + 19.5 * jax.random.uniform(streams_of[4], (CBANDS,), jnp.float32) ** block_levels(streams_of[4], (CBANDS,), ((0, 8),), -0.2, 0.2), 0.5, 20.0),
        "gvec_index": draw_gvec_index(jax.random.fold_in(streams_of[6], 71), 0),
    }


highest = lax.Precision.HIGHEST

def dft_tables(grid_count, freq_count):
    grid_points = jnp.arange(grid_count, dtype=jnp.int32)
    shifted = jnp.arange(freq_count, dtype=jnp.int32) - freq_count // 2
    phase_index = grid_points[:, None] * shifted[None, :] % grid_count
    angles = phase_index.astype(jnp.float32) * (2.0 * math.pi / grid_count)
    scale_factor = 1.0 / math.sqrt(grid_count)
    return (jnp.cos(angles) * scale_factor, -jnp.sin(angles) * scale_factor)

def transform(fields):
    cosine_table, sine_table = dft_tables(NGRID, KB)
    both_tables = jnp.concatenate([cosine_table, sine_table], axis=1)
    zpart = jnp.einsum('vxyz,zq->vxyq', fields, both_tables, precision=highest)
    real_z, imag_z = (zpart[..., :KB], zpart[..., KB:])
    real_y = jnp.einsum('vxyk,yq->vxqk', real_z, cosine_table, precision=highest) - jnp.einsum('vxyk,yq->vxqk', imag_z, sine_table, precision=highest)
    imag_y = jnp.einsum('vxyk,yq->vxqk', imag_z, cosine_table, precision=highest) + jnp.einsum('vxyk,yq->vxqk', real_z, sine_table, precision=highest)
    real_x = jnp.einsum('vxjk,xq->vqjk', real_y, cosine_table, precision=highest) - jnp.einsum('vxjk,xq->vqjk', imag_y, sine_table, precision=highest)
    imag_x = jnp.einsum('vxjk,xq->vqjk', imag_y, cosine_table, precision=highest) + jnp.einsum('vxjk,xq->vqjk', real_y, sine_table, precision=highest)
    return jnp.stack([real_x, imag_x], axis=1)

def reference(valence, conduction, owners, val_energy, cond_energy, gvec_index):
    val_list = [valence[owners[slot], slot].astype(jnp.float32) for slot in range(NV)]
    val_fields = jnp.stack(val_list, axis=0)
    block_index = jnp.arange(NGD * N_GA, dtype=jnp.int32) // NGD
    x_freq = gvec_index // (KYD * KB)
    y_freq = block_index * KYD + gvec_index // KB % KYD
    z_freq = gvec_index % KB
    flat_index = (x_freq * KB * KB + y_freq * KB + z_freq).astype(jnp.int32)

    def one_band(band_wave):
        fields = val_fields * band_wave.astype(jnp.float32)[None]
        spectrum = transform(fields).reshape(NV, 2, KB * KB * KB)
        return spectrum[:, :, flat_index]
    coeffs = lax.map(one_band, conduction)
    coeff_rows = coeffs.reshape(-1, NGD * N_GA).astype(jnp.bfloat16)
    weights = 1.0 / (val_energy[None, :] - cond_energy[:, None])
    col_weights = jnp.repeat(weights.reshape(-1), 2)
    positions = jnp.arange(PANEL_DEV * N_GA, dtype=jnp.int32)
    panel_index = positions // PANEL_DEV * NGD + positions % PANEL_DEV
    chosen = coeff_rows[:, panel_index]
    weighted = (chosen.astype(jnp.float32) * col_weights[:, None]).astype(jnp.bfloat16)
    return lax.dot_general(coeff_rows, weighted, (((0,), (0,)), ((), ())), preferred_element_type=jnp.float32)
```

```python
import functools
import math

import jax
import jax.numpy as jnp
import numpy as np
from jax import lax
from jax.experimental import pallas as pl
from jax.experimental.pallas import tpu as pltpu
from jax.sharding import PartitionSpec as P

KB = 64
PANEL_DEV = 128
SLOTS = 64
CHUNKS = 4

F32 = jnp.float32
BF16 = jnp.bfloat16


def round_up(value, step):
    return -(-value // step) * step


def tables(grid_count):
    grid_points = np.arange(grid_count)
    freqs = np.arange(KB + 1) - KB // 2
    angles = (grid_points[:, None] * freqs[None, :] % grid_count) * (2.0 * math.pi / grid_count)
    scale = 1.0 / math.sqrt(grid_count)
    return np.cos(angles) * scale, -np.sin(angles) * scale


def split_np(values):
    high = np.asarray(values, np.float32).astype(jnp.bfloat16)
    low = (np.asarray(values, np.float64) - high.astype(np.float64)).astype(jnp.bfloat16)
    return high, low


def split(values):
    high = values.astype(BF16)
    return high, (values - high.astype(F32)).astype(BF16)


def mxu(a, b):
    return jnp.dot(a, b, preferred_element_type=F32)


def spectrum_kernel(
    dims, count_ref, group_ref, cond_ref, val_ref, ty_ref, tz_ref, tx_ref, meta_ref, slot_ref,
    out_ref, real_ref, imag_ref,
):
    n_val, n_cond, planes, grid_count, half_pad, stride = dims
    band = pl.program_id(0)
    field_rows = n_val * n_cond * planes

    def one_plane(x, carry):
        wave = cond_ref[0, x].astype(F32)
        pairs = [split(wave * val_ref[k, x].astype(F32)) for k in range(n_val)]
        stacked = jnp.concatenate(
            [
                jnp.concatenate([p[0] for p in pairs], axis=1),
                jnp.concatenate([p[1] for p in pairs], axis=1),
            ],
            axis=0,
        )
        both = mxu(ty_ref[...], stacked)
        both = both[: 2 * half_pad] + both[2 * half_pad :]
        for k in range(n_val):
            row = (k * n_cond + band) * planes + x
            cols = slice(k * grid_count, (k + 1) * grid_count)
            real_ref[pl.ds(row, half_pad, stride=stride), :] = both[:half_pad, cols]
            imag_ref[pl.ds(row, half_pad, stride=stride), :] = both[half_pad:, cols]
        return carry

    lax.fori_loop(0, planes, one_plane, 0, unroll=2)

    @pl.when(band == n_cond - 1)
    def _():
        out_ref[...] = jnp.zeros_like(out_ref)
        lane = lax.broadcasted_iota(jnp.int32, (1, 2 * SLOTS), 1)
        sign = jnp.where(lane < SLOTS, -1.0, 1.0).astype(F32)

        def one_tile(t, carry):
            start = pl.multiple_of(group_ref[t] * stride, 8)
            half = jnp.concatenate(
                [real_ref[pl.ds(start, field_rows), :], imag_ref[pl.ds(start, field_rows), :]], axis=1
            )
            high, low = split(half)
            meta = meta_ref[t]
            pick_z = (lax.broadcasted_iota(jnp.int32, (2 * KB, 2 * SLOTS), 0) == meta[0:1]).astype(F32).astype(BF16)
            turn = meta[2:3].astype(F32)
            basis_high = mxu(tz_ref[0], pick_z)
            basis_low = mxu(tz_ref[1], pick_z)

            def conjugated(basis):
                return jnp.concatenate([basis[:grid_count], basis[grid_count:] * turn], axis=0).astype(BF16)

            basis_high, basis_low = conjugated(basis_high), conjugated(basis_low)
            wide = mxu(high, jnp.concatenate([basis_high, basis_low], axis=1))
            at_g = wide[:, : 2 * SLOTS] + wide[:, 2 * SLOTS :] + mxu(low, basis_high)
            pick_x = (lax.broadcasted_iota(jnp.int32, (KB, 2 * SLOTS), 0) == meta[1:2]).astype(F32).astype(BF16)
            phase = mxu(tx_ref[...], jnp.concatenate([pick_x, pick_x], axis=0))
            rows = phase.shape[0] // 2
            cosine, sine = phase[:rows], phase[rows:] * sign
            turned = pltpu.roll(at_g, SLOTS, axis=1)
            if rows == field_rows:
                moved = at_g * cosine + turned * sine
                field = lax.broadcasted_iota(jnp.int32, (n_val * n_cond, field_rows), 0)
                owner = lax.broadcasted_iota(jnp.int32, (n_val * n_cond, field_rows), 1) // planes
                adder = (field == owner).astype(F32).astype(BF16)
                moved_high, moved_low = split(moved)
                summed = mxu(adder, moved_high) + mxu(adder, moved_low)
            else:
                shape = (n_val * n_cond, planes, 2 * SLOTS)
                moved = at_g.reshape(shape) * cosine[None] + turned.reshape(shape) * sine[None]
                summed = jnp.sum(moved, axis=1)
            n_fields = n_val * n_cond
            fields_pad = out_ref.shape[0] // 2
            summed = jnp.concatenate(
                [summed, jnp.zeros((fields_pad - n_fields, 2 * SLOTS), F32)], axis=0
            )
            parts = jnp.concatenate(
                [summed[:, :SLOTS], pltpu.roll(summed, SLOTS, axis=1)[:, :SLOTS]], axis=0
            )
            parts_high, parts_low = split(parts)
            place = lax.broadcasted_iota(jnp.int32, (SLOTS, slot_ref.shape[1]), 0) + t * SLOTS
            back = (place == slot_ref[...]).astype(F32).astype(BF16)
            placed = mxu(jnp.concatenate([parts_high, parts_low], axis=0), back)
            out_ref[...] += placed[: 2 * fields_pad] + placed[2 * fields_pad :]
            return carry

        lax.fori_loop(0, count_ref[0], one_tile, 0)


def plan_slots(gvec_all, per_block, n_ga):
    n_g = gvec_all.shape[0]
    kyd = KB // n_ga
    n_groups = KB // 2 + 1
    n_tiles = n_groups + -(-n_g // SLOTS)
    block = jnp.arange(n_g, dtype=jnp.int32) // per_block
    q_x = gvec_all // (kyd * KB)
    freq_y = block * kyd + gvec_all // KB % kyd - KB // 2
    q_z = gvec_all % KB
    group = jnp.abs(freq_y)
    member = (jnp.arange(n_groups, dtype=jnp.int32)[:, None] == group[None, :]).astype(jnp.int32)
    counts = jnp.sum(member, axis=1)
    group_tiles = (counts + SLOTS - 1) // SLOTS
    before = jnp.arange(n_groups)[:, None] > jnp.arange(n_groups)[None, :]
    first_tile = jnp.sum(jnp.where(before, group_tiles[None, :], 0), axis=1)
    index = jnp.arange(n_g, dtype=jnp.int32)
    earlier = (group[:, None] == group[None, :]) & (index[:, None] > index[None, :])
    rank = jnp.sum(earlier.astype(jnp.int32), axis=1)
    slot = jnp.sum(member * first_tile[:, None], axis=0) * SLOTS + rank
    packed = (q_x * KB + q_z) * 2 + (freq_y < 0).astype(jnp.int32)
    slots = jnp.arange(n_tiles * SLOTS, dtype=jnp.int32)
    by_slot = jnp.sum(jnp.where(slots[:, None] == slot[None, :], packed[None, :], 0), axis=1)
    by_slot = by_slot.reshape(n_tiles, SLOTS)
    slot_z = by_slot // 2 % KB
    slot_x = by_slot // 2 // KB
    turn = 1 - 2 * (by_slot % 2)
    rows = [
        jnp.concatenate([slot_z, slot_z + KB], axis=1),
        jnp.concatenate([slot_x, slot_x], axis=1),
        jnp.concatenate([turn, turn], axis=1),
    ]
    meta = jnp.stack(rows + [jnp.zeros_like(rows[0])] * 5, axis=1)
    last_tile = first_tile + group_tiles
    tiles = jnp.arange(n_tiles, dtype=jnp.int32)
    tile_group = jnp.sum((last_tile[None, :] <= tiles[:, None]).astype(jnp.int32), axis=1)
    tile_group = jnp.minimum(tile_group, n_groups - 1)
    return jnp.sum(group_tiles).reshape(1), tile_group, meta, slot.reshape(1, n_g)


def gather_blocks(block, n_ga):
    held, hop = block[None], 1
    while hop < n_ga:
        other = lax.ppermute(held, "ga", [(i, i ^ hop) for i in range(n_ga)])
        held = jnp.concatenate([held, other], axis=0)
        hop *= 2
    me, hop = lax.axis_index("ga"), 1
    while hop < n_ga:
        pairs = held.reshape(-1, 2, hop, block.shape[0])
        held = jnp.where(me // hop % 2 == 1, pairs[:, ::-1], pairs)
        hop *= 2
    return held.reshape(-1)


def spread_bands(local, owners, n_band):
    n_val, planes, height, width = local.shape
    me = lax.axis_index("band")
    ring = list(range(0, n_band, 2)) + list(range(n_band - 1, 0, -2))
    place = np.zeros(n_band, np.int32)
    for spot, device in enumerate(ring):
        place[device] = spot
    place = jnp.asarray(place)
    ahead = [(ring[i], ring[(i + 1) % n_band]) for i in range(n_band)]
    behind = [(b, a) for a, b in ahead]
    rows = planes * height
    chunk = rows // (2 * CHUNKS)
    flat = local.reshape(n_val, 2, CHUNKS, chunk, width)
    bands = []
    for k in range(n_val):
        is_root = me == owners[k]
        distance = (place[me] - place[owners[k]]) % n_band
        halves = []
        for way, perm in enumerate((ahead, behind)):
            held, received = None, []
            for step in range(CHUNKS + n_band - 2):
                if held is None:
                    send = flat[k, way, 0]
                elif step < CHUNKS:
                    send = jnp.where(is_root, flat[k, way, step], held)
                else:
                    send = held
                held = lax.ppermute(send, "band", perm)
                received.append(held)
            hops = distance if way == 0 else (n_band - distance) % n_band
            start = jnp.maximum(hops - 1, 0)
            arrived = lax.dynamic_slice_in_dim(jnp.stack(received), start, CHUNKS, 0)
            halves.append(jnp.where(is_root, flat[k, way], arrived))
        bands.append(jnp.stack(halves).reshape(planes, height, width))
    return jnp.stack(bands)


def per_device(valence, conduction, owners, val_energy, cond_energy, gvec_index, *, n_band, n_ga):
    local_val = valence[0]
    n_val = local_val.shape[0]
    n_cond, planes, grid_count, _ = conduction.shape
    n_fields = n_val * n_cond
    field_rows = n_fields * planes
    per_block = gvec_index.shape[0]
    n_g = per_block * n_ga
    half = KB // 2

    gvec_all = gather_blocks(gvec_index, n_ga)
    count, tile_group, meta, slot = plan_slots(gvec_all, per_block, n_ga)
    fields = spread_bands(local_val, owners, n_band)

    cosine, sine = tables(grid_count)
    half_pad = round_up(half + 1, 8)
    stride = round_up(field_rows, 8)
    stride += 8 * (1 - stride // 8 % 2)
    ty = np.zeros((2 * half_pad, grid_count))
    ty[: half + 1] = cosine[:, half:].T
    ty[half_pad : half_pad + half + 1] = sine[:, half:].T
    ty_high, ty_low = split_np(ty)
    ty = np.concatenate([np.tile(ty_high, (1, 2)), np.tile(ty_low, (1, 2))], axis=0)
    cos_z, sin_z = cosine[:, :KB], sine[:, :KB]
    tz = np.stack(split_np(np.block([[cos_z, sin_z], [-sin_z, cos_z]])))
    cos_x = np.concatenate(split_np(cos_z), axis=1)
    sin_x = np.concatenate(split_np(sin_z), axis=1)
    start = lax.axis_index("ga") * planes
    tx = [lax.dynamic_slice_in_dim(jnp.asarray(part), start, planes, 0) for part in (cos_x, sin_x)]
    if planes % 8:
        tx = [jnp.tile(part, (n_fields, 1)) for part in tx]
    tx = jnp.concatenate(tx, axis=0)

    fields_pad = round_up(n_fields, 8)
    whole = lambda shape: pl.BlockSpec(shape, lambda i, *_: (0,) * len(shape))
    partial_sums = pl.pallas_call(
        functools.partial(spectrum_kernel, (n_val, n_cond, planes, grid_count, half_pad, stride)),
        out_shape=jax.ShapeDtypeStruct((2 * fields_pad, n_g), F32),
        grid_spec=pltpu.PrefetchScalarGridSpec(
            num_scalar_prefetch=2,
            grid=(n_cond,),
            in_specs=[
                pl.BlockSpec((1, planes, grid_count, grid_count), lambda i, *_: (i, 0, 0, 0)),
                whole(fields.shape),
                whole(ty.shape),
                whole(tz.shape),
                whole(tx.shape),
                whole(meta.shape),
                whole(slot.shape),
            ],
            out_specs=whole((2 * fields_pad, n_g)),
            scratch_shapes=[pltpu.VMEM((half_pad * stride, grid_count), F32)] * 2,
        ),
        compiler_params=pltpu.CompilerParams(vmem_limit_bytes=48 * 1024 * 1024),
    )(count, tile_group, conduction, fields, jnp.asarray(ty), jnp.asarray(tz), tx, meta, slot)

    total = partial_sums.reshape(2, fields_pad, n_g)[:, :n_fields].reshape(2 * n_fields, n_g)
    hop = 1
    while hop < n_ga:
        total = total + lax.ppermute(total, "ga", [(i, i ^ hop) for i in range(n_ga)])
        hop *= 2
    coeffs = total.astype(BF16)
    weights = 1.0 / (val_energy[:, None] - cond_energy[None, :])
    row_weights = jnp.tile(weights.reshape(-1), 2)
    panel = lax.dynamic_slice_in_dim(coeffs, lax.axis_index("ga") * per_block, PANEL_DEV, 1)
    weighted = (panel.astype(F32) * row_weights[:, None]).astype(BF16)
    rows_per = n_g // n_band
    by_band = coeffs.reshape(2 * n_fields, n_band, rows_per).transpose(1, 0, 2)
    sent = jnp.concatenate(
        [by_band, jnp.broadcast_to(weighted[None], (n_band,) + weighted.shape)], axis=2
    )
    arrived = lax.all_to_all(sent, "band", split_axis=0, concat_axis=0, tiled=True)
    arrived = arrived.reshape(n_band * 2 * n_fields, rows_per + PANEL_DEV)
    return lax.dot_general(
        arrived[:, :rows_per], arrived[:, rows_per:], (((0,), (0,)), ((), ())), preferred_element_type=F32
    )


def solution(mesh):
    in_specs = (
        P("band", None, "ga", None, None),
        P("band", "ga", None, None),
        P(),
        P(),
        P("band"),
        P("ga"),
    )
    body = functools.partial(per_device, n_band=mesh.shape["band"], n_ga=mesh.shape["ga"])
    return jax.shard_map(body, mesh=mesh, in_specs=in_specs, out_specs=P("band", "ga"), check_vma=False)
```
